32 devices in a mesh: row: 8 (over z, x), col: 4 (over y, core).
Axes of the slice: x: 2, y: 2, z: 4, core: 2. Of those that a mesh axis runs over, the one named last changes fastest.
Arguments:
- positions: float32 [3, 8192], P(None, ('row', 'col')), may hold values from 0 to 64, as said below
- forces: float32 [3, 8192], P(None, ('row', 'col')), may hold values from -6 to 6
Outputs:
- velocities: float32 [3, 8192], P(None, ('row', 'col'))
The draws below stay inside these ranges and needn't reach their ends.
Inputs may be any that keep to these rules, and one draw needn't show every extreme that they name: `positions`: the first two coordinates lie within 0 to 64, the third within 0 to 51.
All inputs are finite; a program needn't handle non-finite values.
Results may differ from the reference program's by a relative error of at most 0.0003.
Values sent between devices are 32-bit elements; how exact they have to be, the bound alone decides.
No kernel may reach another device: no remote copies, remote signals or barrier semaphores. Data moves between devices by JAX's collectives and lax.ppermute only.
A program may use at most 64 MiB of HBM per device.

```python
import math
import jax
import jax.numpy as jnp
from jax import lax

BLOBS = 8192
DEPTH = 51


def draw_positions(key, part):
    unit = jax.random.uniform(key, (3, BLOBS), jnp.float32)
    extent = jnp.array([64.0, 64.0, DEPTH * 1.0], jnp.float32).reshape(3, 1)
    return unit * extent


def block_levels(stream_key, dims, shards, smallest, top_value):
    level, own = 1.0, jax.random.fold_in(stream_key, 6)
    for axis_at, blocks in shards:
        steps = jnp.exp(jax.random.uniform(jax.random.fold_in(own, axis_at), (blocks,), jnp.float32, smallest / len(shards), top_value / len(shards)))
        level = level * jnp.repeat(steps, dims[axis_at] // blocks).reshape([-1 if axis == axis_at else 1 for axis in range(len(dims))])
    return level


def centred(own_key, dims, width, bound, pieces=(), kind=jnp.bfloat16):
    entries = jax.random.normal(own_key, dims, jnp.float32) * width
    if len(pieces) > 0:
        entries = block_levels(own_key, dims, pieces, -0.22, 0.18) * entries
    return jnp.clip(entries, min=-bound, max=bound).astype(kind)


def setup_inputs(seed: int = 0) -> dict:
    splits = jax.random.split(jax.random.key(seed), 3)
    return {
        "positions": draw_positions(jax.random.fold_in(splits[2], 71), 0),
        "forces": centred(splits[1], (3, BLOBS), 1.0, 6.0, ((1, 32),), jnp.float32),
    }


mobility_scale = 0.25

def pair_sum(target_pos, source_pos, source_frc):
    offset = target_pos[:, :, None] - source_pos[:, None, :]
    squared = lax.optimization_barrier(jnp.sum(offset * offset, axis=0))
    inverse = lax.rsqrt(jnp.maximum(squared, 1e-12))
    distance = squared * inverse
    near = distance < 2.0
    cubed = inverse * inverse * inverse
    scalar_part = jnp.where(near, 1.0 - 9.0 / 32.0 * distance, 0.75 * inverse + 0.5 * cubed)
    dyad_part = jnp.where(near, 3.0 / 32.0 * inverse, (0.75 * inverse - 1.5 * cubed) * inverse * inverse)
    projected = lax.optimization_barrier(jnp.sum(offset * source_frc[:, None, :], axis=0))
    terms = scalar_part[None] * source_frc[:, None, :] + (dyad_part * projected)[None] * offset
    return lax.optimization_barrier(jnp.sum(terms, axis=2))

def reference(positions, forces):
    blob_count = positions.shape[1]
    target_width = math.gcd(blob_count, 256)
    source_width = math.gcd(blob_count, 2048)
    sources = positions.reshape(3, blob_count // source_width, source_width).transpose(1, 0, 2)
    source_forces = forces.reshape(3, blob_count // source_width, source_width).transpose(1, 0, 2)
    targets = positions.reshape(3, blob_count // target_width, target_width).transpose(1, 0, 2)

    def one_target(target_pos):

        def step(running, source_block):
            return (running + pair_sum(target_pos, source_block[0], source_block[1]), None)
        total, _ = lax.scan(step, jnp.zeros((3, target_width), jnp.float32), (sources, source_forces))
        return total
    blocks = lax.map(one_target, targets)
    return blocks.transpose(1, 0, 2).reshape(3, blob_count) * mobility_scale
```

```python
import functools

import jax
import jax.numpy as jnp
from jax import lax
from jax.experimental import pallas as pl
from jax.experimental.pallas import tpu as pltpu
from jax.sharding import PartitionSpec as P

f32 = jnp.float32
AXES = ("row", "col")
LANES = 128
GROUP = 32
VMEM = pl.BlockSpec(memory_space=pltpu.VMEM)


def pair_terms(target, source):
    dx, dy, dz = target[0] - source[0], target[1] - source[1], target[2] - source[2]
    squared = dx * dx + dy * dy + dz * dz
    inverse = lax.rsqrt(jnp.maximum(squared, 1e-12))
    capped = jnp.minimum(inverse, 0.5)
    q = capped * capped
    mixed = inverse * capped
    scalar = capped * (4.0 - (squared * mixed) * (2.5 - q))
    dyad = (mixed * capped) * (1.5 - 3.0 * q)
    w = dyad * (dx * source[3] + dy * source[4] + dz * source[5])
    return scalar * source[3] + w * dx, scalar * source[4] + w * dy, scalar * source[5] + w * dz


def kernel(count, first, last, tgt_ref, *refs):
    sources = refs[:count]
    prev_ref = None if first else refs[count]
    out_ref = refs[count + (not first)]
    acc_ref = refs[-1] if last else out_ref
    targets = tgt_ref.shape[1]
    columns = jnp.transpose(tgt_ref[...])

    for base in range(0, targets, GROUP):
        target = [
            jnp.broadcast_to(columns[base : base + GROUP, k : k + 1], (GROUP, LANES))
            for k in range(3)
        ]
        if first:
            acc = tuple(jnp.zeros((GROUP, LANES), f32) for _ in range(3))
        else:
            acc = tuple(prev_ref[k, base : base + GROUP, :] for k in range(3))
        for ref in sources:
            blocks, _, width = ref.shape

            def step(i, acc, ref=ref, width=width, target=target):
                for at in range(0, width, LANES):
                    source = [
                        jnp.broadcast_to(ref[i, k : k + 1, at : at + LANES], (GROUP, LANES))
                        for k in range(6)
                    ]
                    acc = tuple(a + t for a, t in zip(acc, pair_terms(target, source)))
                return acc

            acc = lax.fori_loop(0, blocks, step, acc, unroll=min(blocks, 4))
        for k in range(3):
            acc_ref[k, base : base + GROUP, :] = acc[k]
    if last:
        ones = jnp.full((8, LANES), 0.125, f32)
        for k in range(3):
            total = lax.dot_general(
                ones,
                acc_ref[k],
                (((1,), (1,)), ((), ())),
                precision=lax.Precision.HIGHEST,
                preferred_element_type=f32,
            )
            out_ref[k : k + 1, :] = total[0:1, :]


def accumulate(target, sources, prev, last):
    targets = target.shape[1]
    pairs = targets * sum(s.shape[0] * s.shape[2] for s in sources)
    acc_shape = (3, targets, LANES)
    args = [target, *sources] + ([] if prev is None else [prev])
    return pl.pallas_call(
        functools.partial(kernel, len(sources), prev is None, last),
        out_shape=jax.ShapeDtypeStruct((3, targets) if last else acc_shape, f32),
        in_specs=[VMEM] * len(args),
        out_specs=VMEM,
        scratch_shapes=[pltpu.VMEM(acc_shape, f32)] if last else [],
        cost_estimate=pl.CostEstimate(flops=38 * pairs, bytes_accessed=0, transcendentals=pairs),
    )(*args)


def body(sizes, positions, forces):
    devices = sizes[0] * sizes[1]

    def swap(block, bit):
        return lax.ppermute(block, AXES, [(i, i ^ bit) for i in range(devices)])

    bits = []
    bit = devices // 2
    while bit > 1:
        bits.append(bit)
        bit //= 2

    own = jnp.concatenate([positions, forces, jnp.zeros((2, positions.shape[1]), f32)], axis=0)
    target = own
    held = own[None]
    mine, theirs = [held], [swap(held, 1)]
    for bit in bits:
        got = swap(held, bit)
        mine.append(got)
        theirs.append(swap(got, 1))
        held = jnp.concatenate([held, got], axis=0)
    acc = accumulate(target, mine[:-2] + theirs[:-2], None, False)
    acc = accumulate(target, [mine[-2], theirs[-2]], acc, False)
    acc = accumulate(target, [mine[-1]], acc, False)
    return accumulate(target, [theirs[-1]], acc, True)


def solution(mesh):
    sizes = (mesh.shape["row"], mesh.shape["col"])
    return jax.shard_map(
        functools.partial(body, sizes),
        mesh=mesh,
        in_specs=(P(None, AXES), P(None, AXES)),
        out_specs=P(None, AXES),
        check_vma=False,
    )
```

```python
import functools

import jax
import jax.numpy as jnp
from jax import lax
from jax.experimental import pallas as pl
from jax.experimental.pallas import tpu as pltpu
from jax.sharding import PartitionSpec as P

f32 = jnp.float32
AXES = ("row", "col")
LANES = 128
GROUP = 32
VMEM = pl.BlockSpec(memory_space=pltpu.VMEM)


def pair_terms(target, source):
    dx, dy, dz = target[0] - source[0], target[1] - source[1], target[2] - source[2]
    squared = dx * dx + dy * dy + dz * dz
    inverse = lax.rsqrt(jnp.maximum(squared, 1e-12))
    capped = jnp.minimum(inverse, 0.5)
    q = capped * capped
    mixed = inverse * capped
    scalar = capped * (4.0 - (squared * mixed) * (2.5 - q))
    dyad = (mixed * capped) * (1.5 - 3.0 * q)
    w = dyad * (dx * source[3] + dy * source[4] + dz * source[5])
    return scalar * source[3] + w * dx, scalar * source[4] + w * dy, scalar * source[5] + w * dz


def kernel(count, first, last, tgt_ref, *refs):
    sources = refs[:count]
    prev_ref = None if first else refs[count]
    out_ref = refs[count + (not first)]
    acc_ref = refs[-1] if last else out_ref
    targets = tgt_ref.shape[1]
    columns = jnp.transpose(tgt_ref[...])

    for base in range(0, targets, GROUP):
        target = [
            jnp.broadcast_to(columns[base : base + GROUP, k : k + 1], (GROUP, LANES))
            for k in range(3)
        ]
        if first:
            acc = tuple(jnp.zeros((GROUP, LANES), f32) for _ in range(3))
        else:
            acc = tuple(prev_ref[k, base : base + GROUP, :] for k in range(3))
        for ref in sources:
            blocks, _, width = ref.shape

            def step(i, acc, ref=ref, width=width, target=target):
                for at in range(0, width, LANES):
                    source = [
                        jnp.broadcast_to(ref[i, k : k + 1, at : at + LANES], (GROUP, LANES))
                        for k in range(6)
                    ]
                    acc = tuple(a + t for a, t in zip(acc, pair_terms(target, source)))
                return acc

            acc = lax.fori_loop(0, blocks, step, acc, unroll=min(blocks, 4))
        for k in range(3):
            acc_ref[k, base : base + GROUP, :] = acc[k]
    if last:
        ones = jnp.full((8, LANES), 0.125, f32)
        for k in range(3):
            total = lax.dot_general(
                ones,
                acc_ref[k],
                (((1,), (1,)), ((), ())),
                precision=lax.Precision.HIGHEST,
                preferred_element_type=f32,
            )
            out_ref[k : k + 1, :] = total[0:1, :]


def accumulate(target, sources, prev, last):
    targets = target.shape[1]
    pairs = targets * sum(s.shape[0] * s.shape[2] for s in sources)
    acc_shape = (3, targets, LANES)
    args = [target, *sources] + ([] if prev is None else [prev])
    return pl.pallas_call(
        functools.partial(kernel, len(sources), prev is None, last),
        out_shape=jax.ShapeDtypeStruct((3, targets) if last else acc_shape, f32),
        in_specs=[VMEM] * len(args),
        out_specs=VMEM,
        scratch_shapes=[pltpu.VMEM(acc_shape, f32)] if last else [],
        compiler_params=pltpu.CompilerParams(vmem_limit_bytes=8 * 1024 * 1024),
        cost_estimate=pl.CostEstimate(flops=38 * pairs, bytes_accessed=0, transcendentals=pairs),
    )(*args)


def body(sizes, positions, forces):
    devices = sizes[0] * sizes[1]

    def swap(block, bit):
        return lax.ppermute(block, AXES, [(i, i ^ bit) for i in range(devices)])

    bits = []
    bit = devices // 2
    while bit > 1:
        bits.append(bit)
        bit //= 2

    own = jnp.concatenate([positions, forces, jnp.zeros((2, positions.shape[1]), f32)], axis=0)

    held, fresh, acc = own[None], own[None], None
    for step, bit in enumerate(bits):
        late = step == len(bits) - 1
        got = swap(held, bit)
        if late:
            across = swap(held, 1)
            acc = accumulate(own, [fresh], acc, False)
            across, acc = lax.optimization_barrier((across, acc))
            acc = accumulate(own, [across], acc, False)
        elif step > 0:
            acc = accumulate(own, [fresh] if acc is not None else [held], acc, False)
        if acc is not None:
            got, acc = lax.optimization_barrier((got, acc))
        fresh = got
        if not late:
            held = jnp.concatenate([held, got], axis=0)
    across = swap(fresh, 1)
    acc = accumulate(own, [fresh], acc, False)
    across, acc = lax.optimization_barrier((across, acc))
    return accumulate(own, [across], acc, True)


def solution(mesh):
    sizes = (mesh.shape["row"], mesh.shape["col"])
    return jax.shard_map(
        functools.partial(body, sizes),
        mesh=mesh,
        in_specs=(P(None, AXES), P(None, AXES)),
        out_specs=P(None, AXES),
        check_vma=False,
    )
```

```python
import functools

import jax
import jax.numpy as jnp
from jax import lax
from jax.experimental import pallas as pl
from jax.experimental.pallas import tpu as pltpu
from jax.sharding import PartitionSpec as P

f32, bf16 = jnp.float32, jnp.bfloat16
AXES = ("row", "col")
LANES = 128
GROUP = 32
SUMS = 32
CONTRACT_LAST = (((1,), (1,)), ((), ()))
VMEM = pl.BlockSpec(memory_space=pltpu.VMEM)


def pieces(value):
    high = value.astype(bf16).astype(f32)
    rest = value - high
    middle = rest.astype(bf16).astype(f32)
    return high, middle, rest - middle


def halves(value):
    high = value.astype(bf16)
    return high, (value - high.astype(f32)).astype(bf16)


def prepare(tgt_ref, spread_ref, projector_ref):
    target = tgt_ref[...]
    count = target.shape[1]
    columns = jnp.transpose(target)
    for k in range(3):
        spread_ref[k] = jnp.broadcast_to(columns[:, k : k + 1], (count, LANES))
    none = jnp.zeros((3, count), f32)
    high, middle, low = pieces(
        jnp.concatenate(
            [none, 3.0 * target[0:3], jnp.full((1, count), -3.0, f32), none[0:1]], axis=0
        )
    )
    sides = jnp.concatenate([high, high, high, middle, middle, low], axis=0)
    projector_ref[...] = jnp.transpose(sides).astype(bf16)


def add_block(block, row, spread_ref, projector_ref, force_rows, total):
    targets, width = projector_ref.shape[0], row.shape[1]
    along = row[0:3] * row[3:6]
    along = along[0:1] + along[1:2] + along[2:3]
    high, middle, low = pieces(jnp.concatenate([row[0:6], along, row[7:8]], axis=0))
    sides = jnp.concatenate([high, middle, low, high, middle, high], axis=0)
    projection = jnp.dot(projector_ref[...], sides.astype(bf16), preferred_element_type=f32)
    columns = sides[0:SUMS]
    for_scalar = jnp.where(force_rows, columns, 0.0).astype(bf16)
    for_dyad = jnp.where(force_rows, 0.0, columns).astype(bf16)

    parts = [[], [], [], []]
    for base in range(0, targets, GROUP):
        offset = []
        for k in range(3):
            target = spread_ref[k, base : base + GROUP, :]
            target = jnp.concatenate([target] * (width // LANES), axis=1)
            offset.append(target - jnp.broadcast_to(block(k), (GROUP, width)))
        dx, dy, dz = offset
        squared = dx * dx + dy * dy + dz * dz
        along = jnp.where(squared <= 0.0, 0.0, projection[base : base + GROUP])
        inverse = lax.rsqrt(jnp.maximum(squared, 1e-12))
        capped = jnp.minimum(inverse, 0.5)
        q = capped * capped
        mixed = inverse * capped
        scalar = capped * (4.0 - (squared * mixed) * (2.5 - q))
        w = ((mixed * capped) * (0.5 - q)) * along
        for part, value in zip(parts, halves(scalar) + halves(w)):
            part.append(value)
    left = jnp.concatenate([jnp.concatenate(part, axis=0) for part in parts], axis=1)
    right = jnp.concatenate([for_scalar, for_scalar, for_dyad, for_dyad], axis=1)
    half = targets // 2
    return [
        now
        + lax.dot_general(
            left[at : at + half], right, CONTRACT_LAST, preferred_element_type=f32
        )
        for now, at in zip(total, (0, half))
    ]


def kernel(count, first, last, *refs):
    refs = list(refs)
    tgt_ref = refs.pop(0) if first or last else None
    spread_ref, projector_ref = (None, None) if first else (refs.pop(0), refs.pop(0))
    sources = [refs.pop(0) for _ in range(count)]
    prev_ref = None if first else refs.pop(0)
    if first:
        spread_ref, projector_ref = refs.pop(0), refs.pop(0)
        prepare(tgt_ref, spread_ref, projector_ref)
    out_ref = refs.pop(0)
    targets, width = projector_ref.shape[0], sources[0].shape[2]
    half = targets // 2

    index = lax.broadcasted_iota(jnp.int32, (SUMS, width), 0) & 7
    force_rows = (index >= 3) & (index < 6)
    if first:
        total = [jnp.zeros((half, SUMS), f32)] * 2
    else:
        total = [prev_ref[0:half], prev_ref[half:targets]]
    for ref in sources:
        blocks = ref.shape[0]
        together = min(blocks, 8)

        def step(i, total, ref=ref, together=together):
            for j in range(together):
                at = i * together + j
                total = add_block(
                    lambda k: ref[at, k : k + 1, :],
                    ref[at],
                    spread_ref,
                    projector_ref,
                    force_rows,
                    total,
                )
            return total

        if blocks == together:
            total = step(0, total)
        else:
            total = lax.fori_loop(0, blocks // together, step, total)
    if not last:
        out_ref[0:half] = total[0]
        out_ref[half:targets] = total[1]
        return
    wide = jnp.zeros((targets, LANES - SUMS), f32)
    sums = jnp.transpose(jnp.concatenate([jnp.concatenate(total, axis=0), wide], axis=1))
    sums = sums[0:8] + sums[8:16] + sums[16:24]
    out_ref[...] = 0.125 * (sums[3:6] + tgt_ref[0:3] * sums[7:8] - sums[0:3])


def accumulate(target, state, sources, last=False):
    targets = target.shape[1]
    first = state is None
    pairs = targets * sum(s.shape[0] * s.shape[2] for s in sources)
    total = jax.ShapeDtypeStruct((targets, SUMS), f32)
    args = ([target] if first or last else []) + (
        list(sources) if first else [*state[:2], *sources, state[2]]
    )
    if first:
        out = [
            jax.ShapeDtypeStruct((3, targets, LANES), f32),
            jax.ShapeDtypeStruct((targets, 48), bf16),
            total,
        ]
    else:
        out = jax.ShapeDtypeStruct((3, targets), f32) if last else total
    got = pl.pallas_call(
        functools.partial(kernel, len(sources), first, last),
        out_shape=out,
        in_specs=[VMEM] * len(args),
        out_specs=[VMEM] * 3 if first else VMEM,
        compiler_params=pltpu.CompilerParams(vmem_limit_bytes=16 * 1024 * 1024),
        cost_estimate=pl.CostEstimate(flops=38 * pairs, bytes_accessed=0, transcendentals=pairs),
    )(*args)
    if first:
        return tuple(got)
    return got if last else (*state[:2], got)


def body(sizes, positions, forces):
    devices = sizes[0] * sizes[1]

    def swap(block, bit):
        return lax.ppermute(block, AXES, [(i, i ^ bit) for i in range(devices)])

    def after(block, state):
        block, total = lax.optimization_barrier((block, state[2]))
        return block, (*state[:2], total)

    bits = []
    bit = devices // 2
    while bit > 1:
        bits.append(bit)
        bit //= 2

    block = jnp.concatenate([positions, forces, jnp.ones((2, positions.shape[1]), f32)], axis=0)[None]
    own = block[0]
    held, fresh, across, state = block, block, [], None
    for step, bit in enumerate(bits):
        got = swap(held, bit)
        state = accumulate(own, state, [fresh])
        if across:
            across[-1], state = after(across[-1], state)
            state = accumulate(own, state, across)
        got, state = after(got, state)
        across = [swap(got, 1)] if step else [swap(block, 1), swap(got, 1)]
        fresh = got
        if bit != bits[-1]:
            held = jnp.concatenate([held, got], axis=0)
    state = accumulate(own, state, [fresh])
    across[-1], state = after(across[-1], state)
    return accumulate(own, state, across, last=True)


def solution(mesh):
    sizes = (mesh.shape["row"], mesh.shape["col"])
    return jax.shard_map(
        functools.partial(body, sizes),
        mesh=mesh,
        in_specs=(P(None, AXES), P(None, AXES)),
        out_specs=P(None, AXES),
        check_vma=False,
    )
```

```python
import functools

import jax
import jax.numpy as jnp
from jax import lax
from jax.experimental import pallas as pl
from jax.experimental.pallas import tpu as pltpu
from jax.sharding import PartitionSpec as P

f32, bf16 = jnp.float32, jnp.bfloat16
AXES = ("row", "col")
LANES = 128
GROUP = 32
SUMS = 32
CONTRACT_LAST = (((1,), (1,)), ((), ()))
VMEM = pl.BlockSpec(memory_space=pltpu.VMEM)


def pieces(value):
    high = value.astype(bf16).astype(f32)
    rest = value - high
    middle = rest.astype(bf16).astype(f32)
    return high, middle, rest - middle


def halves(value):
    high = value.astype(bf16)
    return high, (value - high.astype(f32)).astype(bf16)


def prepare(tgt_ref, spread_ref, projector_ref):
    target = tgt_ref[...]
    count = target.shape[1]
    columns = jnp.transpose(jnp.concatenate([target, target[0:2]], axis=0))
    for k in range(3):
        spread_ref[k] = jnp.broadcast_to(columns[:, k : k + 1], (count, LANES))
    none = jnp.zeros((3, count), f32)
    high, middle, low = pieces(
        jnp.concatenate(
            [none, 3.0 * target[0:3], jnp.full((1, count), -3.0, f32), none[0:1]], axis=0
        )
    )
    sides = jnp.concatenate([high, high, high, middle, middle, low], axis=0)
    projector_ref[...] = jnp.transpose(sides).astype(bf16)


def add_block(block, row, spread_ref, projector_ref, force_rows, total):
    targets, width = projector_ref.shape[0], row.shape[1]
    along = row[0:3] * row[3:6]
    along = along[0:1] + along[1:2] + along[2:3]
    high, middle, low = pieces(jnp.concatenate([row, along, jnp.ones_like(along)], axis=0))
    sides = jnp.concatenate([high, middle, low, high, middle, high], axis=0)
    projection = jnp.dot(projector_ref[...], sides.astype(bf16), preferred_element_type=f32)
    columns = sides[0:SUMS]
    for_scalar = jnp.where(force_rows, columns, 0.0).astype(bf16)
    for_dyad = jnp.where(force_rows, 0.0, columns).astype(bf16)

    parts = [[], [], [], []]
    for base in range(0, targets, GROUP):
        offset = []
        for k in range(3):
            target = spread_ref[k, base : base + GROUP, :]
            target = jnp.concatenate([target] * (width // LANES), axis=1)
            offset.append(target - jnp.broadcast_to(block(k), (GROUP, width)))
        dx, dy, dz = offset
        squared = dx * dx + dy * dy + dz * dz
        along = jnp.where(squared <= 0.0, 0.0, projection[base : base + GROUP])
        inverse = lax.rsqrt(jnp.maximum(squared, 2.25e-12))
        capped = jnp.minimum(inverse, 1.0 / 3.0)
        q = capped * capped
        mixed = inverse * capped
        scalar = capped * ((q + 5.0 / 3.0) - squared * mixed)
        w = ((mixed * capped) * (2.0 / 9.0 - q)) * along
        for part, value in zip(parts, halves(scalar) + halves(w)):
            part.append(value)
    left = jnp.concatenate([jnp.concatenate(part, axis=0) for part in parts], axis=1)
    right = jnp.concatenate([for_scalar, for_scalar, for_dyad, for_dyad], axis=1)
    half = targets // 2
    return [
        now
        + lax.dot_general(
            left[at : at + half], right, CONTRACT_LAST, preferred_element_type=f32
        )
        for now, at in zip(total, (0, half))
    ]


def kernel(count, first, last, *refs):
    refs = list(refs)
    tgt_ref = refs.pop(0) if first or last else None
    spread_ref, projector_ref = (None, None) if first else (refs.pop(0), refs.pop(0))
    sources = [refs.pop(0) for _ in range(count)]
    prev_ref = None if first else refs.pop(0)
    if first:
        spread_ref, projector_ref = refs.pop(0), refs.pop(0)
        prepare(tgt_ref, spread_ref, projector_ref)
    out_ref = refs.pop(0)
    targets, width = projector_ref.shape[0], sources[0].shape[2]
    half = targets // 2

    index = lax.broadcasted_iota(jnp.int32, (SUMS, width), 0) & 7
    force_rows = (index >= 3) & (index < 6)
    if first:
        total = [jnp.zeros((half, SUMS), f32)] * 2
    else:
        total = [prev_ref[0:half], prev_ref[half:targets]]
    for ref in sources:
        blocks = ref.shape[0]
        together = min(blocks, 8)

        def step(i, total, ref=ref, together=together):
            for j in range(together):
                at = i * together + j
                total = add_block(
                    lambda k: ref[at, k : k + 1, :],
                    ref[at],
                    spread_ref,
                    projector_ref,
                    force_rows,
                    total,
                )
            return total

        if blocks == together:
            total = step(0, total)
        else:
            total = lax.fori_loop(0, blocks // together, step, total)
    if not last:
        out_ref[0:half] = total[0]
        out_ref[half:targets] = total[1]
        return
    wide = jnp.zeros((targets, LANES - SUMS), f32)
    sums = jnp.transpose(jnp.concatenate([jnp.concatenate(total, axis=0), wide], axis=1))
    sums = sums[0:8] + sums[8:16] + sums[16:24]
    out_ref[...] = 0.421875 * (sums[3:6] + tgt_ref[0:3] * sums[7:8] - sums[0:3])


def accumulate(target, state, sources, last=False):
    targets = target.shape[1]
    first = state is None
    pairs = targets * sum(s.shape[0] * s.shape[2] for s in sources)
    total = jax.ShapeDtypeStruct((targets, SUMS), f32)
    args = ([target] if first or last else []) + (
        list(sources) if first else [*state[:2], *sources, state[2]]
    )
    if first:
        out = [
            jax.ShapeDtypeStruct((3, targets, LANES), f32),
            jax.ShapeDtypeStruct((targets, 48), bf16),
            total,
        ]
    else:
        out = jax.ShapeDtypeStruct((3, targets), f32) if last else total
    got = pl.pallas_call(
        functools.partial(kernel, len(sources), first, last),
        out_shape=out,
        in_specs=[VMEM] * len(args),
        out_specs=[VMEM] * 3 if first else VMEM,
        compiler_params=pltpu.CompilerParams(vmem_limit_bytes=16 * 1024 * 1024),
        cost_estimate=pl.CostEstimate(flops=38 * pairs, bytes_accessed=0, transcendentals=pairs),
    )(*args)
    if first:
        return tuple(got)
    return got if last else (*state[:2], got)


def body(sizes, positions, forces):
    devices = sizes[0] * sizes[1]

    def swap(block, bit):
        return lax.ppermute(block, AXES, [(i, i ^ bit) for i in range(devices)])

    def after(block, state):
        block, total = lax.optimization_barrier((block, state[2]))
        return block, (*state[:2], total)

    bits = []
    bit = devices // 2
    while bit > 1:
        bits.append(bit)
        bit //= 2

    block = jnp.concatenate([1.5 * positions, forces], axis=0)[None]
    own = block[0]
    held, fresh, state = block, block, None
    for step, bit in enumerate(bits):
        got = swap(held, bit | 1)
        known = len(bits) - step - 1
        if known == 1:
            across = swap(held, 1)
        state = accumulate(own, state, [fresh])
        if known < 2:
            across, state = after(across, state)
            state = accumulate(own, state, [across])
        got, state = after(got, state)
        if known < 2:
            across = swap(got, 1)
        fresh = got
        if known:
            held = jnp.concatenate([held, got], axis=0)
    state = accumulate(own, state, [fresh])
    across, state = after(across, state)
    return accumulate(own, state, [across], last=True)


def solution(mesh):
    sizes = (mesh.shape["row"], mesh.shape["col"])
    return jax.shard_map(
        functools.partial(body, sizes),
        mesh=mesh,
        in_specs=(P(None, AXES), P(None, AXES)),
        out_specs=P(None, AXES),
        check_vma=False,
    )
```

```python
import functools

import jax
import jax.numpy as jnp
from jax import lax
from jax.experimental import pallas as pl
from jax.experimental.pallas import tpu as pltpu
from jax.sharding import PartitionSpec as P

f32, bf16 = jnp.float32, jnp.bfloat16
AXES = ("row", "col")
LANES = 128
GROUP = 32
SUMS = 32
CONTRACT_LAST = (((1,), (1,)), ((), ()))
VMEM = pl.BlockSpec(memory_space=pltpu.VMEM)


def pieces(value):
    high = value.astype(bf16).astype(f32)
    rest = value - high
    middle = rest.astype(bf16).astype(f32)
    return high, middle, rest - middle


def halves(value):
    high = value.astype(bf16)
    return high, (value - high.astype(f32)).astype(bf16)


def prepare(tgt_ref, spread_ref, projector_ref):
    target = tgt_ref[...]
    count = target.shape[1]
    columns = jnp.transpose(jnp.concatenate([target, target[0:2]], axis=0))
    for k in range(3):
        spread_ref[k] = jnp.broadcast_to(columns[:, k : k + 1], (count, LANES))
    none = jnp.zeros((3, count), f32)
    high, middle, low = pieces(
        jnp.concatenate(
            [none, 3.0 * target[0:3], jnp.full((1, count), -3.0, f32), none[0:1]], axis=0
        )
    )
    sides = jnp.concatenate([high, high, high, middle, middle, low], axis=0)
    projector_ref[...] = jnp.transpose(sides).astype(bf16)


def add_block(block, row, spread_ref, projector_ref, total):
    targets, width = projector_ref.shape[0], row.shape[1]
    along = row[0:3] * row[3:6]
    along = along[0:1] + along[1:2] + along[2:3]
    high, middle, low = pieces(jnp.concatenate([row, along, jnp.ones_like(along)], axis=0))
    sides = jnp.concatenate([high, middle, low, high, middle, high], axis=0)
    projection = jnp.dot(projector_ref[...], sides.astype(bf16), preferred_element_type=f32)
    columns = sides[0:SUMS]
    side = columns.astype(bf16)
    side = jnp.concatenate([side, side], axis=1)

    parts = [[], [], [], []]
    for base in range(0, targets, GROUP):
        offset = []
        for k in range(3):
            target = spread_ref[k, base : base + GROUP, :]
            target = jnp.concatenate([target] * (width // LANES), axis=1)
            offset.append(target - jnp.broadcast_to(block(k), (GROUP, width)))
        dx, dy, dz = offset
        squared = dx * dx + dy * dy + dz * dz
        along = jnp.where(squared <= 0.0, 0.0, projection[base : base + GROUP])
        inverse = lax.rsqrt(jnp.maximum(squared, 2.25e-12))
        capped = jnp.minimum(inverse, 1.0 / 3.0)
        q = capped * capped
        mixed = inverse * capped
        scalar = capped * ((q + 5.0 / 3.0) - squared * mixed)
        w = ((mixed * capped) * (2.0 / 9.0 - q)) * along
        for part, value in zip(parts, halves(scalar) + halves(w)):
            part.append(value)
    parts = [jnp.concatenate(part, axis=0) for part in parts]
    half = targets // 2
    sums = []
    for now, (pair, at) in zip(total, [(p, at) for p in (parts[:2], parts[2:]) for at in (0, half)]):
        sums.append(
            now
            + lax.dot_general(
                jnp.concatenate([part[at : at + half] for part in pair], axis=1),
                side,
                CONTRACT_LAST,
                preferred_element_type=f32,
            )
        )
    return sums


def kernel(count, first, last, *refs):
    refs = list(refs)
    tgt_ref = refs.pop(0) if first or last else None
    spread_ref, projector_ref = (None, None) if first else (refs.pop(0), refs.pop(0))
    sources = [refs.pop(0) for _ in range(count)]
    prev_ref = None if first else refs.pop(0)
    if first:
        spread_ref, projector_ref = refs.pop(0), refs.pop(0)
        prepare(tgt_ref, spread_ref, projector_ref)
    out_ref = refs.pop(0)
    targets = projector_ref.shape[0]
    half = targets // 2

    if first:
        total = [jnp.zeros((half, SUMS), f32)] * 4
    else:
        total = [prev_ref[i * half : i * half + half] for i in range(4)]
    for ref in sources:
        blocks = ref.shape[0]
        together = min(blocks, 8)

        def step(i, total, ref=ref, together=together):
            for j in range(together):
                at = i * together + j
                total = add_block(
                    lambda k: ref[at, k : k + 1, :],
                    ref[at],
                    spread_ref,
                    projector_ref,
                    total,
                )
            return total

        if blocks == together:
            total = step(0, total)
        else:
            total = lax.fori_loop(0, blocks // together, step, total)
    if not last:
        for i in range(4):
            out_ref[i * half : i * half + half] = total[i]
        return
    wide = jnp.zeros((targets, LANES - SUMS), f32)
    lane = lax.broadcasted_iota(jnp.int32, (targets, SUMS), 1) & 7
    scalar_sums, dyad_sums = (jnp.concatenate(total[i : i + 2], axis=0) for i in (0, 2))
    total = jnp.where((lane >= 3) & (lane < 6), scalar_sums, dyad_sums)
    sums = jnp.transpose(jnp.concatenate([total, wide], axis=1))
    sums = sums[0:8] + sums[8:16] + sums[16:24]
    out_ref[...] = 0.421875 * (sums[3:6] + tgt_ref[0:3] * sums[7:8] - sums[0:3])


def accumulate(target, state, sources, last=False):
    targets = target.shape[1]
    first = state is None
    pairs = targets * sum(s.shape[0] * s.shape[2] for s in sources)
    total = jax.ShapeDtypeStruct((2 * targets, SUMS), f32)
    args = ([target] if first or last else []) + (
        list(sources) if first else [*state[:2], *sources, state[2]]
    )
    if first:
        out = [
            jax.ShapeDtypeStruct((3, targets, LANES), f32),
            jax.ShapeDtypeStruct((targets, 48), bf16),
            total,
        ]
    else:
        out = jax.ShapeDtypeStruct((3, targets), f32) if last else total
    got = pl.pallas_call(
        functools.partial(kernel, len(sources), first, last),
        out_shape=out,
        in_specs=[VMEM] * len(args),
        out_specs=[VMEM] * 3 if first else VMEM,
        compiler_params=pltpu.CompilerParams(vmem_limit_bytes=16 * 1024 * 1024),
        cost_estimate=pl.CostEstimate(flops=38 * pairs, bytes_accessed=0, transcendentals=pairs),
    )(*args)
    if first:
        return tuple(got)
    return got if last else (*state[:2], got)


def body(sizes, positions, forces):
    devices = sizes[0] * sizes[1]

    def swap(block, bit):
        return lax.ppermute(block, AXES, [(i, i ^ bit) for i in range(devices)])

    def after(block, state):
        block, total = lax.optimization_barrier((block, state[2]))
        return block, (*state[:2], total)

    bits = []
    bit = devices // 2
    while bit > 1:
        bits.append(bit)
        bit //= 2

    block = jnp.concatenate([1.5 * positions, forces], axis=0)[None]
    own = block[0]
    held, fresh, state = block, block, None
    for step, bit in enumerate(bits):
        got = swap(held, bit | 1)
        known = len(bits) - step - 1
        if known == 1:
            across = swap(held, 1)
        state = accumulate(own, state, [fresh])
        if known < 2:
            across, state = after(across, state)
            state = accumulate(own, state, [across])
        got, state = after(got, state)
        if known < 2:
            across = swap(got, 1)
        fresh = got
        if known:
            held = jnp.concatenate([held, got], axis=0)
    state = accumulate(own, state, [fresh])
    across, state = after(across, state)
    return accumulate(own, state, [across], last=True)


def solution(mesh):
    sizes = (mesh.shape["row"], mesh.shape["col"])
    return jax.shard_map(
        functools.partial(body, sizes),
        mesh=mesh,
        in_specs=(P(None, AXES), P(None, AXES)),
        out_specs=P(None, AXES),
        check_vma=False,
    )
```

```python
import functools

import jax
import jax.numpy as jnp
from jax import lax
from jax.experimental import pallas as pl
from jax.experimental.pallas import tpu as pltpu
from jax.sharding import PartitionSpec as P

f32, bf16 = jnp.float32, jnp.bfloat16
AXES = ("row", "col")
LANES = 128
GROUP = 32
SUMS = 32
CONTRACT_LAST = (((1,), (1,)), ((), ()))
VMEM = pl.BlockSpec(memory_space=pltpu.VMEM)


def pieces(value):
    high = value.astype(bf16).astype(f32)
    rest = value - high
    middle = rest.astype(bf16).astype(f32)
    return high, middle, rest - middle


def halves(value):
    high = value.astype(bf16)
    return high, (value - high.astype(f32)).astype(bf16)


def prepare(tgt_ref, spread_ref, projector_ref):
    target = tgt_ref[...]
    count = target.shape[1]
    columns = jnp.transpose(jnp.concatenate([target, target[0:2]], axis=0))
    for k in range(3):
        spread_ref[k] = jnp.broadcast_to(columns[:, k : k + 1], (count, LANES))
    none = jnp.zeros((3, count), f32)
    high, middle, low = pieces(
        jnp.concatenate(
            [none, 3.0 * target[0:3], jnp.full((1, count), -3.0, f32), none[0:1]], axis=0
        )
    )
    sides = jnp.concatenate([high, high, high, middle, middle, low], axis=0)
    projector_ref[...] = jnp.transpose(sides).astype(bf16)


def add_block(block, row, spread_ref, projector_ref, total):
    targets, width = projector_ref.shape[0], row.shape[1]
    along = row[0:3] * row[3:6]
    along = along[0:1] + along[1:2] + along[2:3]
    high, middle, low = pieces(jnp.concatenate([row, along, jnp.ones_like(along)], axis=0))
    sides = jnp.concatenate([high, middle, low, high, middle, high], axis=0)
    projection = jnp.dot(projector_ref[...], sides.astype(bf16), preferred_element_type=f32)
    columns = sides[0:SUMS]
    side = columns.astype(bf16)
    side = jnp.concatenate([side, side], axis=1)

    parts = [[], [], [], []]
    for base in range(0, targets, GROUP):
        offset = []
        for k in range(3):
            target = spread_ref[k, base : base + GROUP, :]
            target = jnp.concatenate([target] * (width // LANES), axis=1)
            offset.append(target - jnp.broadcast_to(block(k), (GROUP, width)))
        dx, dy, dz = offset
        squared = dx * dx + dy * dy + dz * dz
        along = jnp.where(squared <= 0.0, 0.0, projection[base : base + GROUP])
        inverse = lax.rsqrt(jnp.maximum(squared, 2.25e-12))
        capped = jnp.minimum(inverse, 1.0 / 3.0)
        q = capped * capped
        mixed = inverse * capped
        scalar = capped * ((q + 5.0 / 3.0) - squared * mixed)
        w = ((mixed * capped) * (2.0 / 9.0 - q)) * along
        for part, value in zip(parts, halves(scalar) + halves(w)):
            part.append(value)
    parts = [jnp.concatenate(part, axis=0) for part in parts]
    half = targets // 2
    sums = []
    for now, (pair, at) in zip(total, [(p, at) for p in (parts[:2], parts[2:]) for at in (0, half)]):
        sums.append(
            now
            + lax.dot_general(
                jnp.concatenate([part[at : at + half] for part in pair], axis=1),
                side,
                CONTRACT_LAST,
                preferred_element_type=f32,
            )
        )
    return sums


def kernel(count, first, last, *refs):
    refs = list(refs)
    tgt_ref = refs.pop(0) if first or last else None
    spread_ref, projector_ref = (None, None) if first else (refs.pop(0), refs.pop(0))
    sources = [refs.pop(0) for _ in range(count)]
    prev_ref = None if first else refs.pop(0)
    if first:
        spread_ref, projector_ref = refs.pop(0), refs.pop(0)
        prepare(tgt_ref, spread_ref, projector_ref)
    out_ref = refs.pop(0)
    targets = projector_ref.shape[0]
    half = targets // 2

    if first:
        total = [jnp.zeros((half, SUMS), f32)] * 4
    else:
        total = [prev_ref[i * half : i * half + half] for i in range(4)]
    for ref in sources:
        blocks = ref.shape[0]
        together = min(blocks, 8)

        def step(i, total, ref=ref, together=together):
            for j in range(together):
                at = i * together + j
                total = add_block(
                    lambda k: ref[at, k : k + 1, :],
                    ref[at],
                    spread_ref,
                    projector_ref,
                    total,
                )
            return total

        if blocks == together:
            total = step(0, total)
        else:
            total = lax.fori_loop(0, blocks // together, step, total)
    if not last:
        for i in range(4):
            out_ref[i * half : i * half + half] = total[i]
        return
    wide = jnp.zeros((targets, LANES - SUMS), f32)
    lane = lax.broadcasted_iota(jnp.int32, (targets, SUMS), 1) & 7
    scalar_sums, dyad_sums = (jnp.concatenate(total[i : i + 2], axis=0) for i in (0, 2))
    total = jnp.where((lane >= 3) & (lane < 6), scalar_sums, dyad_sums)
    sums = jnp.transpose(jnp.concatenate([total, wide], axis=1))
    sums = sums[0:8] + sums[8:16] + sums[16:24]
    out_ref[...] = 0.421875 * (sums[3:6] + tgt_ref[0:3] * sums[7:8] - sums[0:3])


def accumulate(target, state, sources, last=False):
    targets = target.shape[1]
    first = state is None
    pairs = targets * sum(s.shape[0] * s.shape[2] for s in sources)
    total = jax.ShapeDtypeStruct((2 * targets, SUMS), f32)
    args = ([target] if first or last else []) + (
        list(sources) if first else [*state[:2], *sources, state[2]]
    )
    if first:
        out = [
            jax.ShapeDtypeStruct((3, targets, LANES), f32),
            jax.ShapeDtypeStruct((targets, 48), bf16),
            total,
        ]
    else:
        out = jax.ShapeDtypeStruct((3, targets), f32) if last else total
    got = pl.pallas_call(
        functools.partial(kernel, len(sources), first, last),
        out_shape=out,
        in_specs=[VMEM] * len(args),
        out_specs=[VMEM] * 3 if first else VMEM,
        compiler_params=pltpu.CompilerParams(vmem_limit_bytes=16 * 1024 * 1024),
        cost_estimate=pl.CostEstimate(flops=38 * pairs, bytes_accessed=0, transcendentals=pairs),
    )(*args)
    if first:
        return tuple(got)
    return got if last else (*state[:2], got)


def body(sizes, positions, forces):
    devices = sizes[0] * sizes[1]

    def swap(block, bit):
        return lax.ppermute(block, AXES, [(i, i ^ bit) for i in range(devices)])

    def after(block, state):
        block, total = lax.optimization_barrier((block, state[2]))
        return block, (*state[:2], total)

    bits = []
    bit = devices // 2
    while bit > 1:
        bits.append(bit)
        bit //= 2

    block = jnp.concatenate([1.5 * positions, forces], axis=0)[None]
    own = block[0]
    held, fresh, state = block, block, None
    for step, bit in enumerate(bits):
        got = swap(held, bit | 1)
        known = len(bits) - step - 1
        if known == 1:
            across = swap(held, 1)
        state = accumulate(own, state, [fresh, across] if known == 1 else [fresh])
        if known == 0:
            across, state = after(across, state)
            state = accumulate(own, state, [across])
        got, state = after(got, state)
        if known < 2:
            across = swap(got, 1)
        fresh = got
        if known:
            held = jnp.concatenate([held, got], axis=0)
    state = accumulate(own, state, [fresh])
    across, state = after(across, state)
    return accumulate(own, state, [across], last=True)


def solution(mesh):
    sizes = (mesh.shape["row"], mesh.shape["col"])
    return jax.shard_map(
        functools.partial(body, sizes),
        mesh=mesh,
        in_specs=(P(None, AXES), P(None, AXES)),
        out_specs=P(None, AXES),
        check_vma=False,
    )
```
